256 devices in a mesh: blk: 32 (over y_hi, z, core), grp: 8 (over y_lo, x).
Axes of the slice: x: 4, y: 4 (y_hi: 2, y_lo: 2; y = y_hi * 2 + y_lo), z: 8, core: 2. Of those that a mesh axis runs over, the one named last changes fastest.
Arguments:
- images: bfloat16 [16384, 1152], P(('blk', 'grp')), may hold values from -0.1875 to 0.1875
- texts: bfloat16 [16384, 1152], P(('blk', 'grp')), may hold values from -0.1875 to 0.1875
- logit_scale: float32 [1], replicated, may hold values from 4 to 16
- logit_bias: float32 [1], replicated, may hold values from -6 to -4
Outputs:
- image_grad: float32 [16384, 1152], P(('blk', 'grp'))
- text_grad: float32 [16384, 1152], P(('blk', 'grp'))
The draws below stay inside these ranges and needn't reach their ends.
All inputs are finite; a program needn't handle non-finite values.
Results may differ from the reference program's by a relative error of at most 0.015.
Values may be sent and summed in bfloat16 or wider, within the bound.
No kernel may reach another device: no remote copies, remote signals or barrier semaphores. Data moves between devices by JAX's collectives and lax.ppermute only.
A program may use at most 64 MiB of HBM per device.

```python
import math
import jax
import jax.numpy as jnp
from jax import lax

D = 1152
PAIRS = 16384


def block_scale(stream_key, extent, cuts, low, high):
    def one(position, parts):
        heights = jax.random.uniform(jax.random.fold_in(jax.random.fold_in(stream_key, 6), position), (parts,), jnp.float32, low / len(cuts), high / len(cuts))
        return jnp.repeat(jnp.exp(heights), extent[position] // parts).reshape((-1,) + (1,) * (len(extent) - position - 1))

    factor_of = one(*cuts[0])
    for cut in cuts[1:]:
        factor_of = factor_of * one(*cut)
    return factor_of


def bell_draw(key, extent, deviation, most, split=(), kind=jnp.bfloat16):
    drawn = jax.random.normal(key, extent, jnp.float32) * deviation
    if len(split) > 0:
        drawn = block_scale(key, extent, split, -0.22, 0.18) * drawn
    return jnp.clip(drawn, min=-most, max=most).astype(kind)


def setup_inputs(seed: int = 0) -> dict:
    splits = jax.random.split(jax.random.key(seed), 5)
    return {
        "images": bell_draw(splits[0], (PAIRS, D), D ** -0.5, 0.1875, ((0, 256),)),
        "texts": bell_draw(splits[1], (PAIRS, D), D ** -0.5, 0.1875, ((0, 256),)),
        "logit_scale": jnp.clip(jnp.exp(jax.random.uniform(splits[2], (1,), jnp.float32, math.log(4.0), math.log(16.0))), 4.0, 16.0),
        "logit_bias": jnp.clip(jax.random.uniform(splits[3], (1,), jnp.float32, -6.0, -4.0), -6.0, -4.0),
    }


epsilon = 1e-06

def unit_rows(values):
    widened = values.astype(jnp.float32)
    inverse = lax.rsqrt(lax.optimization_barrier(jnp.sum(widened * widened, axis=1, keepdims=True)) + epsilon)
    return (widened * inverse, inverse)

def through_norm(unit_part, inverse, along_unit):
    projected = lax.optimization_barrier(jnp.sum(unit_part * along_unit, axis=1, keepdims=True))
    return (along_unit - unit_part * projected) * inverse

def tile_terms(text_block, text_rows, image_block, image_rows, factor, offset):
    logits = lax.dot_general(text_block, image_block, (((1,), (1,)), ((), ())), preferred_element_type=jnp.float32)
    logits = factor * logits + offset
    paired = (text_rows[:, None] == image_rows[None, :]).astype(jnp.float32)
    weights = (factor * (jax.nn.sigmoid(logits) - paired)).astype(jnp.bfloat16)
    image_part = lax.dot_general(weights, text_block, (((0,), (0,)), ((), ())), preferred_element_type=jnp.float32)
    text_part = jnp.dot(weights, image_block, preferred_element_type=jnp.float32)
    return (image_part, text_part)

def reference(images, texts, logit_scale, logit_bias):
    factor = logit_scale[0]
    offset = logit_bias[0]
    image_unit, image_inverse = unit_rows(images)
    text_unit, text_inverse = unit_rows(texts)
    image_send = image_unit.astype(jnp.bfloat16)
    text_send = text_unit.astype(jnp.bfloat16)
    total_rows = images.shape[0]
    block_rows = math.gcd(total_rows, 512)
    image_rows = jnp.arange(total_rows, dtype=jnp.int32)

    def one_block(image_total, first):
        text_block = lax.dynamic_slice_in_dim(text_send, first, block_rows, 0)
        text_rows = first + jnp.arange(block_rows, dtype=jnp.int32)
        image_part, text_part = tile_terms(text_block, text_rows, image_send, image_rows, factor, offset)
        return (image_total + image_part, text_part)
    starts = jnp.arange(0, total_rows, block_rows, dtype=jnp.int32)
    image_total, text_parts = lax.scan(one_block, jnp.zeros(images.shape, jnp.float32), starts)
    text_total = text_parts.reshape(total_rows, images.shape[1])
    image_grad = through_norm(image_unit, image_inverse, image_total)
    text_grad = through_norm(text_unit, text_inverse, text_total)
    return (image_grad, text_grad)
```

```python
import jax
import jax.numpy as jnp
from jax import lax
from jax.sharding import PartitionSpec as P

epsilon = 1e-06
AXES = ("blk", "grp")


def place(x, y, z, core):
    return ((((y >> 1) * 8 + z) * 2 + core) * 2 + (y & 1)) * 4 + x


def partner(position, size, first):
    step = 1 if (position % 2 == 0) == first else -1
    return (position + step) % size


def pairs_of(axis, first):
    pairs = []
    for x in range(4):
        for y in range(4):
            for z in range(8):
                for core in range(2):
                    side = first == (core == 0)
                    to = [x, y, z, core]
                    if axis == "x":
                        to[0] = partner(x, 4, side)
                    elif axis == "y":
                        to[1] = partner(y, 4, side)
                    elif axis == "z":
                        to[2] = partner(z, 8, side)
                    else:
                        to[3] = 1 - core
                    pairs.append((place(x, y, z, core), place(*to)))
    return sorted(pairs)


def exchange(axis, first=True):
    pairs = pairs_of(axis, first)
    return lambda value: lax.ppermute(value, AXES, pairs)


def unit_rows(values):
    widened = values.astype(jnp.float32)
    inverse = lax.rsqrt(jnp.sum(widened * widened, axis=1, keepdims=True) + epsilon)
    return (widened * inverse, inverse)


def through_norm(unit_part, inverse, along_unit):
    projected = jnp.sum(unit_part * along_unit, axis=1, keepdims=True)
    return (along_unit - unit_part * projected) * inverse


def tile_terms(texts, images, factor, offset):
    logits = lax.dot_general(
        texts, images, (((1,), (1,)), ((), ())), preferred_element_type=jnp.float32
    )
    weights = (factor * jax.nn.sigmoid(factor * logits + offset)).astype(jnp.bfloat16)
    image_part = lax.dot_general(
        weights, texts, (((0,), (0,)), ((), ())), preferred_element_type=jnp.float32
    )
    text_part = jnp.dot(weights, images, preferred_element_type=jnp.float32)
    return (image_part, text_part)


def rounded(value):
    return value.astype(jnp.bfloat16)


def widened(value):
    return value.astype(jnp.float32)


def join(*parts):
    return jnp.concatenate(parts, axis=0)


def local(images, texts, logit_scale, logit_bias):
    x1, x2 = exchange("x", True), exchange("x", False)
    y1, y2 = exchange("y", True), exchange("y", False)
    z1, z2 = exchange("z", True), exchange("z", False)
    sibling = exchange("core")
    route_a = (x1, x2, y1, y2)
    route_b = (y1, y2, x1, x2)
    half = images.shape[0] // 2
    factor = logit_scale[0]
    offset = logit_bias[0]
    image_unit, image_inverse = unit_rows(images)
    text_unit, text_inverse = unit_rows(texts)
    image_send = rounded(image_unit)
    text_send = rounded(text_unit)

    a, b = image_send[:half], image_send[half:]
    t0 = text_send
    r1 = z1(t0)
    a = join(a, route_a[0](a))
    b = join(b, route_b[0](b))
    near = join(t0, r1)
    r2 = z2(near)
    a = join(a, route_a[1](a))
    b = join(b, route_b[1](b))
    r3 = z1(r2)
    a = join(a, route_a[2](a))
    b = join(b, route_b[2](b))
    first_text = join(near, r2)
    first_other = sibling(first_text)
    r4 = z2(r3)
    late_a = route_a[3](a)
    late_b = route_b[3](b)
    second_text = join(r3, r4)
    second_other = sibling(second_text)
    all_texts = join(first_text, second_text, first_other, second_other)

    early_images = join(a, b)
    late_images = join(late_a, late_b)
    early_sum, text_early = tile_terms(all_texts, early_images, factor, offset)
    late_sum, text_late = tile_terms(all_texts, late_images, factor, offset)
    text_sum = text_early + text_late

    count = early_images.shape[0] // 2
    keep_a, keep_b = early_sum[:count], early_sum[count:]
    give_a, give_b = late_sum[:count], late_sum[count:]
    own_texts = t0.shape[0] * 8
    column = text_sum[:own_texts] + widened(sibling(rounded(text_sum[own_texts:])))
    s0, s1 = column[:64], column[64:128]
    s2, s3, s4 = column[128:256], column[256:384], column[384:]
    for step in (3, 2, 1, 0):
        keep_a = keep_a + widened(route_a[step](rounded(give_a)))
        keep_b = keep_b + widened(route_b[step](rounded(give_b)))
        if step > 0:
            count = count // 2
            keep_a, give_a = keep_a[:count], keep_a[count:]
            keep_b, give_b = keep_b[:count], keep_b[count:]
    s3 = s3 + widened(z2(rounded(s4)))
    s2 = s2 + widened(z1(rounded(s3)))
    s01 = join(s0, s1) + widened(z2(rounded(s2)))
    text_total = s01[:64] + widened(z1(rounded(s01[64:])))
    image_total = join(keep_a, keep_b) - factor * widened(text_send)
    text_total = text_total - factor * widened(image_send)
    image_grad = through_norm(image_unit, image_inverse, image_total)
    text_grad = through_norm(text_unit, text_inverse, text_total)
    return (image_grad, text_grad)


def solution(mesh):
    in_specs = (P(AXES, None), P(AXES, None), P(), P())
    out_specs = (P(AXES, None), P(AXES, None))
    return jax.shard_map(local, mesh=mesh, in_specs=in_specs, out_specs=out_specs, check_vma=False)
```

```python
import functools

import jax
import jax.numpy as jnp
from jax import lax
from jax.experimental import pallas as pl
from jax.experimental.pallas import tpu as pltpu
from jax.sharding import PartitionSpec as P

epsilon = 1e-06
log2_e = 1.4426950408889634
AXES = ("blk", "grp")


def place(x, y, z, core):
    return ((((y >> 1) * 8 + z) * 2 + core) * 2 + (y & 1)) * 4 + x


def partner(position, size, first):
    step = 1 if (position % 2 == 0) == first else -1
    return (position + step) % size


def pairs_of(axis, first):
    pairs = []
    for x in range(4):
        for y in range(4):
            for z in range(8):
                for core in range(2):
                    side = first == (core == 0)
                    to = [x, y, z, core]
                    if axis == "x":
                        to[0] = partner(x, 4, side)
                    elif axis == "y":
                        to[1] = partner(y, 4, side)
                    elif axis == "z":
                        to[2] = partner(z, 8, side)
                    else:
                        to[3] = 1 - core
                    pairs.append((place(x, y, z, core), place(*to)))
    return sorted(pairs)


def exchange(axis, first=True):
    hops = [dict(pairs_of(one, first)) for one in ((axis,) if axis == "core" else axis)]
    pairs = []
    for source in sorted(hops[0]):
        target = source
        for hop in hops:
            target = hop[target]
        pairs.append((source, target))
    return lambda value: lax.ppermute(value, AXES, pairs)


def unit_rows(values):
    widened = values.astype(jnp.float32)
    inverse = lax.rsqrt(jnp.sum(widened * widened, axis=1, keepdims=True) + epsilon)
    return (widened * inverse, inverse)


def through_norm(unit_part, inverse, along_unit):
    projected = jnp.sum(unit_part * along_unit, axis=1, keepdims=True)
    return (along_unit - unit_part * projected) * inverse


def rounded(value):
    return value.astype(jnp.bfloat16)


def widened(value):
    return value.astype(jnp.float32)


def join(*parts):
    return jnp.concatenate(parts, axis=0)


def send_kernel(rows, *rest):
    rest[-1][...] = rounded(unit_rows(rows[...])[0])


def send_rows(rows, *earlier):
    whole = pl.BlockSpec(memory_space=pltpu.VMEM)
    return pl.pallas_call(
        send_kernel,
        out_shape=jax.ShapeDtypeStruct(rows.shape, jnp.bfloat16),
        in_specs=[whole] * (1 + len(earlier)),
        out_specs=whole,
        compiler_params=pltpu.CompilerParams(vmem_limit_bytes=4 * 2**20),
    )(rows, *earlier)


def grad_kernel(factor, rows, others, sums, *rest):
    *arrived, grad = rest
    unit, inverse = unit_rows(rows[...])
    other_send = widened(rounded(unit_rows(others[...])[0]))
    total = sums[...] - factor[0] * other_send
    for part in arrived:
        total = total + widened(part[...])
    grad[...] = through_norm(unit, inverse, total)


def grad_rows(factor, rows, others, sums, *arrived):
    whole = pl.BlockSpec(memory_space=pltpu.VMEM)
    return pl.pallas_call(
        grad_kernel,
        out_shape=jax.ShapeDtypeStruct(rows.shape, jnp.float32),
        in_specs=[pl.BlockSpec(memory_space=pltpu.SMEM)] + [whole] * (3 + len(arrived)),
        out_specs=whole,
        compiler_params=pltpu.CompilerParams(vmem_limit_bytes=4 * 2**20),
    )(factor, rows, others, sums, *arrived)


def weights_of(factor, offset, texts, images):
    logits = lax.dot_general(
        texts[...], images[...], (((1,), (1,)), ((), ())), preferred_element_type=jnp.float32
    )
    decay = jnp.exp2(logits * (factor * -log2_e) + offset * -log2_e)
    return rounded(factor / (1.0 + decay))


def for_images(weights, texts):
    return lax.dot_general(
        weights, texts[...], (((0,), (0,)), ((), ())), preferred_element_type=jnp.float32
    )


def for_texts(weights, images):
    return jnp.dot(weights, images[...], preferred_element_type=jnp.float32)


def rows_of(*refs):
    return jnp.concatenate([ref[...] for ref in refs], axis=0)


def columns_of(*parts):
    return jnp.concatenate(parts, axis=1)


def weight_kernel(count, scale, bias, *refs):
    *inputs, weights = refs
    weights[...] = weights_of(
        scale[0], bias[0], rows_of(*inputs[:count]), rows_of(*inputs[count:])
    )


def corner_kernel(scale, bias, own_a, sib_a, own_b, sib_b, quad, part_x, part_y, part_d,
                  w_aq, w_axy, w_bqxy, w_d, sums_own, sums_own_b, send):
    a, b = own_a.shape[0], own_b.shape[0]
    w_d[...] = weights_of(scale[0], bias[0], rows_of(own_a, sib_a, own_b, sib_b), part_d)
    images = rows_of(quad, part_x, part_y, part_d)
    late = w_d[pl.ds(2 * a, 2 * b)]
    total = for_texts(columns_of(w_bqxy[...], late), images)
    sums_own_b[...] = total[:b]
    send[pl.ds(0, b)] = rounded(total[b:])
    late = w_d[pl.ds(0, 2 * a)]
    total = for_texts(columns_of(w_aq[...], w_axy[...], late), images)
    sums_own[...] = total[:a]
    send[pl.ds(b, a)] = rounded(total[a:])


def sibling_kernel(scale, bias, sib_c, quad, part_x, part_y, part_d, weights, send):
    images = rows_of(quad, part_x, part_y, part_d)
    weights[...] = weights_of(scale[0], bias[0], sib_c, images)
    send[...] = rounded(for_texts(weights[...], images))


def text_kernel(weights, quad, part_x, part_y, part_d, sums):
    sums[...] = for_texts(weights[...], rows_of(quad, part_x, part_y, part_d))


def image_kernel(count, *refs):
    *inputs, sums = refs
    total = for_images(rows_of(*inputs[:count]), rows_of(*inputs[count:]))
    sums[...] = total.astype(sums.dtype)


def on_device(kernel, outputs, *operands, scalars=0, products=0):
    vmem = pl.BlockSpec(memory_space=pltpu.VMEM)
    smem = pl.BlockSpec(memory_space=pltpu.SMEM)
    width = operands[-1].shape[-1]
    return pl.pallas_call(
        kernel,
        out_shape=[jax.ShapeDtypeStruct(shape, kind) for shape, kind in outputs],
        in_specs=[smem] * scalars + [vmem] * (len(operands) - scalars),
        out_specs=[vmem] * len(outputs),
        compiler_params=pltpu.CompilerParams(vmem_limit_bytes=16 * 2**20),
        cost_estimate=pl.CostEstimate(
            flops=2 * width * products, bytes_accessed=0, transcendentals=0
        ),
    )(*operands)


def after(value, *others):
    return lax.optimization_barrier((value,) + others)[0]


def local(images, texts, logit_scale, logit_bias):
    x1, y1, d1 = exchange("x", True), exchange("y", True), exchange("xy", True)
    x2, y2, d2 = exchange("x", False), exchange("y", False), exchange("xy", False)
    z1, z2 = exchange("z", True), exchange("z", False)
    sibling = exchange("core")
    f32, bf16 = jnp.float32, jnp.bfloat16
    n, d = images.shape
    a, b, q = 4 * n, 2 * n, 4 * n
    scalars = (logit_scale, logit_bias)
    text_send = send_rows(texts)
    image_send = send_rows(images, text_send)

    def weigh(some_texts, some_images, share=1):
        m = sum(v.shape[0] for v in some_texts)
        k = sum(v.shape[0] for v in some_images)
        return on_device(
            functools.partial(weight_kernel, len(some_texts)), [((m, k), bf16)],
            *scalars, *some_texts, *some_images, scalars=2, products=share * m * k,
        )[0]

    r1 = z1(text_send)
    quad = join(image_send, x1(image_send), y1(image_send), d1(image_send))
    near = join(text_send, r1)
    r2 = z2(near)
    part_x, part_y, part_d = x2(quad), y2(quad), d2(quad)
    r3 = z1(r2)
    own_a = join(near, r2)
    sib_a = sibling(own_a)
    w_aq = weigh((own_a, sib_a), (quad,))
    w_axy = weigh((own_a, sib_a), (part_x, part_y), share=40)
    r3 = after(r3, w_aq, w_axy)
    r4 = z2(r3)
    sib_b = sibling(r3)
    w_bqxy = weigh((r3, sib_b), (quad, part_x, part_y))
    w_d, sums_own, sums_own_b, send_ab = on_device(
        corner_kernel,
        [((2 * a + 2 * b, q), bf16), ((a, d), f32), ((b, d), f32), ((a + b, d), bf16)],
        *scalars, own_a, sib_a, r3, sib_b, quad, part_x, part_y, part_d, w_aq, w_axy, w_bqxy,
        scalars=2, products=40 * 3 * q * (a + b),
    )
    r4 = after(r4, send_ab)
    back_ab = sibling(send_ab)
    all_images = (quad, part_x, part_y, part_d)
    sib_c = sibling(r4)
    w_own = weigh((r4,), all_images)
    w_sib, send_c = on_device(
        sibling_kernel, [((b, 4 * q), bf16), ((b, d), bf16)], *scalars, sib_c, *all_images,
        scalars=2, products=2 * b * 4 * q,
    )
    (sums_own_c,) = on_device(
        text_kernel, [((b, d), f32)], w_own, *all_images, products=b * 4 * q
    )
    s4 = rounded(sums_own_c + widened(sibling(send_c)))
    all_texts = (own_a, sib_a, r3, sib_b, r4, sib_c)

    def image_part(kind, *blocks):
        return on_device(
            functools.partial(image_kernel, len(blocks)), [((q, d), kind)],
            *blocks, *all_texts, products=q * 8 * q // 2,
        )[0]

    def late(index, *others):
        span = slice(index * q, (index + 1) * q)
        return after(w_own[:, span], *others), w_sib[:, span]

    back_d = d2(image_part(bf16, w_d, *late(3)))
    back_x = x2(image_part(bf16, w_axy[:, :q], w_bqxy[:, q : 2 * q], *late(1, s4)))
    back_y = y2(image_part(bf16, w_axy[:, q:], w_bqxy[:, 2 * q :], *late(2, s4)))
    s4 = z2(s4)
    quad_sums = image_part(f32, w_aq, w_bqxy[:, :q], *late(0, s4))
    s3 = sums_own_b + widened(back_ab[:b]) + widened(s4)
    near_sums = sums_own + widened(back_ab[b:])
    s2 = near_sums[2 * n :] + widened(z1(rounded(s3)))
    s01 = near_sums[: 2 * n] + widened(z2(rounded(s2)))
    quad_sums = quad_sums + widened(back_d) + widened(back_x) + widened(back_y)
    text_grad = grad_rows(logit_scale, texts, images, s01[:n], z1(rounded(s01[n:])))
    image_grad = grad_rows(
        logit_scale,
        images,
        texts,
        quad_sums[:n],
        d1(rounded(quad_sums[3 * n :])),
        x1(rounded(quad_sums[n : 2 * n])),
        y1(rounded(quad_sums[2 * n : 3 * n])),
    )
    return (image_grad, text_grad)


def solution(mesh):
    in_specs = (P(AXES, None), P(AXES, None), P(), P())
    out_specs = (P(AXES, None), P(AXES, None))
    return jax.shard_map(local, mesh=mesh, in_specs=in_specs, out_specs=out_specs, check_vma=False)
```

```python
import functools

import jax
import jax.numpy as jnp
from jax import lax
from jax.experimental import pallas as pl
from jax.experimental.pallas import tpu as pltpu
from jax.sharding import PartitionSpec as P

epsilon = 1e-06
log2_e = 1.4426950408889634
AXES = ("blk", "grp")


def place(x, y, z, core):
    return ((((y >> 1) * 8 + z) * 2 + core) * 2 + (y & 1)) * 4 + x


def partner(position, size, first):
    step = 1 if (position % 2 == 0) == first else -1
    return (position + step) % size


def pairs_of(axis, first):
    pairs = []
    for x in range(4):
        for y in range(4):
            for z in range(8):
                for core in range(2):
                    side = first == (core == 0)
                    to = [x, y, z, core]
                    if axis == "x":
                        to[0] = partner(x, 4, side)
                    elif axis == "y":
                        to[1] = partner(y, 4, side)
                    elif axis == "z":
                        to[2] = partner(z, 8, side)
                    else:
                        to[3] = 1 - core
                    pairs.append((place(x, y, z, core), place(*to)))
    return sorted(pairs)


def exchange(axis, first=True):
    hops = [dict(pairs_of(one, first)) for one in ((axis,) if axis == "core" else axis)]
    pairs = []
    for source in sorted(hops[0]):
        target = source
        for hop in hops:
            target = hop[target]
        pairs.append((source, target))
    return lambda value: lax.ppermute(value, AXES, pairs)


def unit_rows(values):
    widened = values.astype(jnp.float32)
    inverse = lax.rsqrt(jnp.sum(widened * widened, axis=1, keepdims=True) + epsilon)
    return (widened * inverse, inverse)


def through_norm(unit_part, inverse, along_unit):
    projected = jnp.sum(unit_part * along_unit, axis=1, keepdims=True)
    return (along_unit - unit_part * projected) * inverse


def rounded(value):
    return value.astype(jnp.bfloat16)


def widened(value):
    return value.astype(jnp.float32)


def join(*parts):
    return jnp.concatenate(parts, axis=0)


def send_kernel(rows, *rest):
    rest[-1][...] = rounded(unit_rows(rows[...])[0])


def send_rows(rows, *earlier):
    whole = pl.BlockSpec(memory_space=pltpu.VMEM)
    return pl.pallas_call(
        send_kernel,
        out_shape=jax.ShapeDtypeStruct(rows.shape, jnp.bfloat16),
        in_specs=[whole] * (1 + len(earlier)),
        out_specs=whole,
        compiler_params=pltpu.CompilerParams(vmem_limit_bytes=4 * 2**20),
    )(rows, *earlier)


def grad_kernel(coefficients, rows, others, sums, *rest):
    *arrived, grad = rest
    unit, inverse = unit_rows(rows[...])
    other_send = widened(rounded(unit_rows(others[...])[0]))
    total = sums[...] - scale_and_bias(coefficients)[0] * other_send
    for part in arrived:
        total = total + widened(part[...])
    grad[...] = through_norm(unit, inverse, total)


def grad_rows(coefficients, rows, others, sums, *arrived):
    whole = pl.BlockSpec(memory_space=pltpu.VMEM)
    return pl.pallas_call(
        grad_kernel,
        out_shape=jax.ShapeDtypeStruct(rows.shape, jnp.float32),
        in_specs=[whole] * (4 + len(arrived)),
        out_specs=whole,
        compiler_params=pltpu.CompilerParams(vmem_limit_bytes=4 * 2**20),
    )(coefficients, rows, others, sums, *arrived)


def weights_of(factor, offset, texts, images):
    logits = lax.dot_general(
        texts[...], images[...], (((1,), (1,)), ((), ())), preferred_element_type=jnp.float32
    )
    decay = jnp.exp2(logits * (factor * -log2_e) + offset * -log2_e)
    return rounded(factor / (1.0 + decay))


def for_images(weights, texts):
    return lax.dot_general(
        weights, texts[...], (((0,), (0,)), ((), ())), preferred_element_type=jnp.float32
    )


def for_texts(weights, images):
    return jnp.dot(weights, images[...], preferred_element_type=jnp.float32)


def scale_and_bias(coefficients):
    return coefficients[0:1, 0:1], coefficients[4:5, 0:1]


def rows_of(*refs):
    return jnp.concatenate([ref[...] for ref in refs], axis=0)


def columns_of(*parts):
    return jnp.concatenate(parts, axis=1)


def weight_kernel(count, coefficients, *refs):
    *inputs, weights = refs
    weights[...] = weights_of(
        *scale_and_bias(coefficients), rows_of(*inputs[:count]), rows_of(*inputs[count:])
    )


def near_kernel(count, *refs):
    *inputs, sums_own, send = refs
    weights = columns_of(*[ref[...] for ref in inputs[:count]])
    total = for_texts(weights, rows_of(*inputs[count:]))
    own = sums_own.shape[0]
    sums_own[...] = total[:own]
    send[...] = rounded(total[own:])


def sibling_kernel(coefficients, sib_c, quad, part_x, part_y, top_d, low_d, weights, send):
    images = rows_of(quad, part_x, part_y, top_d, low_d)
    weights[...] = weights_of(*scale_and_bias(coefficients), sib_c, images)
    send[...] = rounded(for_texts(weights[...], images))


def text_kernel(weights, *refs):
    *images, sums = refs
    sums[...] = for_texts(weights[...], rows_of(*images))


def image_kernel(count, *refs):
    *inputs, sums = refs
    total = for_images(rows_of(*inputs[:count]), rows_of(*inputs[count:]))
    sums[...] = total.astype(sums.dtype)


def on_device(kernel, outputs, *operands, products=0):
    vmem = pl.BlockSpec(memory_space=pltpu.VMEM)
    width = operands[-1].shape[-1]
    return pl.pallas_call(
        kernel,
        out_shape=[jax.ShapeDtypeStruct(shape, kind) for shape, kind in outputs],
        in_specs=[vmem] * len(operands),
        out_specs=[vmem] * len(outputs),
        compiler_params=pltpu.CompilerParams(vmem_limit_bytes=16 * 2**20),
        cost_estimate=pl.CostEstimate(
            flops=2 * width * products, bytes_accessed=0, transcendentals=0
        ),
    )(*operands)


def after(value, *others):
    return lax.optimization_barrier((value,) + others)[0]


def local(images, texts, logit_scale, logit_bias):
    x1, y1, d1 = exchange("x", True), exchange("y", True), exchange("xy", True)
    x2, y2, d2 = exchange("x", False), exchange("y", False), exchange("xy", False)
    z1, z2 = exchange("z", True), exchange("z", False)
    sibling = exchange("core")
    f32, bf16 = jnp.float32, jnp.bfloat16
    n, d = images.shape
    a, b, q = 4 * n, 2 * n, 4 * n
    coefficients = join(*[jnp.broadcast_to(v, (4, 128)) for v in (logit_scale, logit_bias)])
    text_send = send_rows(texts)
    image_send = send_rows(images, text_send)

    def weigh(some_texts, some_images, share=1):
        m = sum(v.shape[0] for v in some_texts)
        k = sum(v.shape[0] for v in some_images)
        return on_device(
            functools.partial(weight_kernel, len(some_texts)), [((m, k), bf16)],
            coefficients, *some_texts, *some_images, products=share * m * k,
        )[0]

    r1 = z1(text_send)
    quad = join(image_send, after(x1(image_send), coefficients), y1(image_send), d1(image_send))
    pair = join(text_send, r1)
    r2 = z2(pair)
    part_x, part_y = x2(quad), y2(quad)
    r3 = z1(r2)
    top_d, low_d = y2(part_x[: q // 2]), x2(part_y[q // 2 :])
    r4 = z2(r3)
    own_a = join(pair, r2)
    sib_a = sibling(own_a)
    w_aq = weigh((own_a, sib_a), (quad,))
    w_axy = weigh((own_a, sib_a), (part_x, part_y))
    sib_b = sibling(r3)
    w_bqxy = weigh((r3, sib_b), (quad, part_x, part_y))
    w_d = weigh((after(own_a, w_aq, w_axy, w_bqxy), sib_a, r3, sib_b), (top_d, low_d), share=40)
    all_images = (quad, part_x, part_y, top_d, low_d)

    def near(rows, *blocks, products=0):
        return on_device(
            functools.partial(near_kernel, len(blocks)), [((rows, d), f32), ((rows, d), bf16)],
            *blocks, *all_images, products=products,
        )

    sums_own_b, send_b = near(b, w_bqxy, w_d[2 * a :], products=40 * 2 * b * 4 * q)
    r4 = after(r4, send_b)
    back_b = sibling(send_b)
    sib_c = sibling(r4)
    w_own = weigh((r4,), all_images)
    w_sib, send_c = on_device(
        sibling_kernel, [((b, 4 * q), bf16), ((b, d), bf16)], coefficients, sib_c, *all_images,
        products=2 * b * 4 * q,
    )
    (sums_own_c,) = on_device(
        text_kernel, [((b, d), f32)], w_own, *all_images, products=b * 4 * q
    )
    s4 = rounded(sums_own_c + widened(sibling(send_c)))
    all_texts = (own_a, sib_a, r3, sib_b, r4, sib_c)

    def image_part(kind, *blocks, share=1):
        return on_device(
            functools.partial(image_kernel, len(blocks)), [((q, d), kind)],
            *blocks, *all_texts, products=share * q * 4 * q,
        )[0]

    def late(index, *others):
        span = slice(index * q, (index + 1) * q)
        return after(w_own[:, span], *others), w_sib[:, span]

    back_d = d2(image_part(bf16, w_d, *late(3)))
    send_x = image_part(bf16, w_axy[:, :q], w_bqxy[:, q : 2 * q], *late(1, s4))
    send_y = image_part(bf16, w_axy[:, q:], w_bqxy[:, 2 * q :], *late(2, s4))
    back_x, back_y = x2(send_x), y2(send_y)
    sums_own, send_a = near(a, after(w_aq, s4), w_axy, w_d[: 2 * a], products=2 * a * 4 * q)
    back_a = sibling(send_a)
    s4 = after(z2(s4), send_a)
    s3 = sums_own_b + widened(back_b) + widened(s4)
    near_sums = sums_own + widened(back_a)
    s2 = near_sums[2 * n :] + widened(z1(rounded(s3)))
    quad_sums = image_part(f32, w_aq, w_bqxy[:, :q], *late(0, s2), share=1)
    s01 = near_sums[: 2 * n] + widened(z2(rounded(s2)))
    quad_sums = quad_sums + widened(back_d) + widened(back_x) + widened(back_y)
    text_grad = grad_rows(coefficients, texts, images, s01[:n], z1(rounded(s01[n:])))
    image_grad = grad_rows(
        coefficients,
        images,
        texts,
        quad_sums[:n],
        d1(rounded(quad_sums[3 * n :])),
        x1(rounded(quad_sums[n : 2 * n])),
        y1(rounded(quad_sums[2 * n : 3 * n])),
    )
    return (image_grad, text_grad)


def solution(mesh):
    in_specs = (P(AXES, None), P(AXES, None), P(), P())
    out_specs = (P(AXES, None), P(AXES, None))
    return jax.shard_map(local, mesh=mesh, in_specs=in_specs, out_specs=out_specs, check_vma=False)
```

```python
import functools

import jax
import jax.numpy as jnp
from jax import lax
from jax.experimental import pallas as pl
from jax.experimental.pallas import tpu as pltpu
from jax.sharding import PartitionSpec as P

epsilon = 1e-06
log2_e = 1.4426950408889634
AXES = ("blk", "grp")


def place(x, y, z, core):
    return ((((y >> 1) * 8 + z) * 2 + core) * 2 + (y & 1)) * 4 + x


def partner(position, size, first):
    step = 1 if (position % 2 == 0) == first else -1
    return (position + step) % size


def pairs_of(axis, first):
    pairs = []
    for x in range(4):
        for y in range(4):
            for z in range(8):
                for core in range(2):
                    side = first == (core == 0)
                    to = [x, y, z, core]
                    if axis == "x":
                        to[0] = partner(x, 4, side)
                    elif axis == "y":
                        to[1] = partner(y, 4, side)
                    elif axis == "z":
                        to[2] = partner(z, 8, side)
                    else:
                        to[3] = 1 - core
                    pairs.append((place(x, y, z, core), place(*to)))
    return sorted(pairs)


def exchange(axis, first=True):
    hops = [dict(pairs_of(one, first)) for one in ((axis,) if axis == "core" else axis)]
    pairs = []
    for source in sorted(hops[0]):
        target = source
        for hop in hops:
            target = hop[target]
        pairs.append((source, target))
    return lambda value: lax.ppermute(value, AXES, pairs)


def unit_rows(values):
    widened = values.astype(jnp.float32)
    inverse = lax.rsqrt(jnp.sum(widened * widened, axis=1, keepdims=True) + epsilon)
    return (widened * inverse, inverse)


def through_norm(unit_part, inverse, along_unit):
    projected = jnp.sum(unit_part * along_unit, axis=1, keepdims=True)
    return (along_unit - unit_part * projected) * inverse


def rounded(value):
    return value.astype(jnp.bfloat16)


def widened(value):
    return value.astype(jnp.float32)


def join(*parts):
    return jnp.concatenate(parts, axis=0)


def unit_kernel(rows, units):
    units[...] = rounded(unit_rows(rows[...])[0])


def block_kernel(own, *refs):
    *arrived, block = refs
    n = own.shape[0]
    block[pl.ds(0, n)] = own[...]
    for index, rows in enumerate(arrived):
        block[pl.ds((index + 1) * n, n)] = rounded(unit_rows(rows[...])[0])


def grad_kernel(coefficients, rows, others, sums, *rest):
    *arrived, grad = rest
    unit, inverse = unit_rows(rows[...])
    other_send = widened(rounded(unit_rows(others[...])[0]))
    total = sums[...] - scale_and_bias(coefficients)[0] * other_send
    for part in arrived:
        total = total + widened(part[...])
    grad[...] = through_norm(unit, inverse, total)


def grad_rows(coefficients, rows, others, sums, *arrived):
    whole = pl.BlockSpec(memory_space=pltpu.VMEM)
    return pl.pallas_call(
        grad_kernel,
        out_shape=jax.ShapeDtypeStruct(rows.shape, jnp.float32),
        in_specs=[whole] * (4 + len(arrived)),
        out_specs=whole,
        compiler_params=pltpu.CompilerParams(vmem_limit_bytes=4 * 2**20),
    )(coefficients, rows, others, sums, *arrived)


def weights_of(factor, offset, texts, images):
    logits = lax.dot_general(
        texts[...], images[...], (((1,), (1,)), ((), ())), preferred_element_type=jnp.float32
    )
    decay = jnp.exp2(logits * (factor * -log2_e) + offset * -log2_e)
    return rounded(factor / (1.0 + decay))


def for_images(weights, texts):
    return lax.dot_general(
        weights, texts[...], (((0,), (0,)), ((), ())), preferred_element_type=jnp.float32
    )


def for_texts(weights, images):
    return jnp.dot(weights, images[...], preferred_element_type=jnp.float32)


def scale_and_bias(coefficients):
    return coefficients[0:1, 0:1], coefficients[4:5, 0:1]


def rows_of(*refs):
    return jnp.concatenate([ref[...] for ref in refs], axis=0)


def columns_of(*parts):
    return jnp.concatenate(parts, axis=1)


def weight_kernel(count, coefficients, *refs):
    *inputs, weights = refs
    weights[...] = weights_of(
        *scale_and_bias(coefficients), rows_of(*inputs[:count]), rows_of(*inputs[count:])
    )


def near_kernel(count, *refs):
    *inputs, sums_own, send = refs
    weights = columns_of(*[ref[...] for ref in inputs[:count]])
    total = for_texts(weights, rows_of(*inputs[count:]))
    own = sums_own.shape[0]
    sums_own[...] = total[:own]
    send[...] = rounded(total[own:])


def sibling_kernel(coefficients, sib_c, quad, part_x, part_y, top_d, low_d, weights, send):
    images = rows_of(quad, part_x, part_y, top_d, low_d)
    weights[...] = weights_of(*scale_and_bias(coefficients), sib_c, images)
    send[...] = rounded(for_texts(weights[...], images))


def text_kernel(weights, *refs):
    *images, sums = refs
    sums[...] = for_texts(weights[...], rows_of(*images))


def image_kernel(count, *refs):
    *inputs, sums = refs
    total = for_images(rows_of(*inputs[:count]), rows_of(*inputs[count:]))
    sums[...] = total.astype(sums.dtype)


def on_device(kernel, outputs, *operands, products=0):
    vmem = pl.BlockSpec(memory_space=pltpu.VMEM)
    width = operands[-1].shape[-1]
    return pl.pallas_call(
        kernel,
        out_shape=[jax.ShapeDtypeStruct(shape, kind) for shape, kind in outputs],
        in_specs=[vmem] * len(operands),
        out_specs=[vmem] * len(outputs),
        compiler_params=pltpu.CompilerParams(vmem_limit_bytes=16 * 2**20),
        cost_estimate=pl.CostEstimate(
            flops=2 * width * products, bytes_accessed=0, transcendentals=0
        ),
    )(*operands)


def after(value, *others):
    return lax.optimization_barrier((value,) + others)[0]


def local(images, texts, logit_scale, logit_bias):
    x1, y1, d1 = exchange("x", True), exchange("y", True), exchange("xy", True)
    x2, y2, d2 = exchange("x", False), exchange("y", False), exchange("xy", False)
    z1, z2 = exchange("z", True), exchange("z", False)
    sibling = exchange("core")
    f32, bf16 = jnp.float32, jnp.bfloat16
    n, d = images.shape
    a, b, q = 4 * n, 2 * n, 4 * n
    coefficients = join(*[jnp.broadcast_to(v, (4, 128)) for v in (logit_scale, logit_bias)])
    coefficients = join(*[jnp.broadcast_to(v, (4, 128)) for v in (logit_scale, logit_bias)])

    def units_of(rows):
        return on_device(unit_kernel, [((n, d), bf16)], rows)[0]

    def block_of(own, *arrived):
        return on_device(block_kernel, [(((1 + len(arrived)) * n, d), bf16)], own, *arrived)[0]

    def weigh(some_texts, some_images, share=1):
        m = sum(v.shape[0] for v in some_texts)
        k = sum(v.shape[0] for v in some_images)
        return on_device(
            functools.partial(weight_kernel, len(some_texts)), [((m, k), bf16)],
            coefficients, *some_texts, *some_images, products=share * m * k,
        )[0]

    raw = (d1(images), x1(images), y1(images), z1(texts), units_of(texts), units_of(images), coefficients)
    raw_d, raw_x, raw_y, raw_t, own_text, own_image, coefficients = lax.optimization_barrier(raw)
    pair = block_of(own_text, raw_t)
    quad = block_of(own_image, raw_x, raw_y, raw_d)
    r2 = z2(pair)
    part_x, part_y = x2(quad), y2(quad)
    r3 = z1(r2)
    top_d, low_d = y2(part_x[: q // 2]), x2(part_y[q // 2 :])
    r4 = z2(r3)
    own_a = join(pair, r2)
    sib_a = sibling(own_a)
    w_aq = weigh((own_a, sib_a), (quad,), share=0)
    w_axy = weigh((own_a, sib_a), (part_x, part_y), share=0)
    w_ad = weigh((after(own_a, w_aq, w_axy), sib_a), (top_d, low_d), share=40)
    sib_b = sibling(r3)
    all_images = (quad, part_x, part_y, top_d, low_d)

    def near(rows, *blocks, products=0):
        return on_device(
            functools.partial(near_kernel, len(blocks)), [((rows, d), f32), ((rows, d), bf16)],
            *blocks, *all_images, products=products,
        )

    w_b = weigh((after(r3, w_ad), sib_b), all_images)
    sums_own_b, send_b = near(b, w_b, products=2 * b * 4 * q)
    r4 = after(r4, send_b)
    back_b = sibling(send_b)
    sib_c = sibling(r4)
    w_own = weigh((r4,), all_images)
    w_sib, send_c = on_device(
        sibling_kernel, [((b, 4 * q), bf16), ((b, d), bf16)], coefficients, sib_c, *all_images,
        products=2 * b * 4 * q,
    )
    (sums_own_c,) = on_device(
        text_kernel, [((b, d), f32)], w_own, *all_images, products=b * 4 * q
    )
    back_c = sibling(send_c)
    all_texts = (own_a, sib_a, r3, sib_b, r4, sib_c)

    def image_part(kind, *blocks, share=1):
        return on_device(
            functools.partial(image_kernel, len(blocks)), [((q, d), kind)],
            *blocks, *all_texts, products=share * q * 4 * q,
        )[0]

    def late(index, *others):
        span = slice(index * q, (index + 1) * q)
        return after(w_b[:, span], *others), w_own[:, span], w_sib[:, span]

    send_d = image_part(bf16, w_ad, *late(3))
    back_d = d2(send_d)
    s4 = rounded(after(sums_own_c, send_d) + widened(back_c))
    send_x = image_part(bf16, w_axy[:, :q], *late(1, s4))
    send_y = image_part(bf16, w_axy[:, q:], *late(2, s4))
    back_x, back_y = x2(send_x), y2(send_y)
    sums_own, send_a = near(a, after(w_aq, s4), w_axy, w_ad, products=2 * a * 4 * q)
    back_a = sibling(send_a)
    s4 = after(z2(s4), send_a)
    s3 = sums_own_b + widened(back_b) + widened(s4)
    near_sums = sums_own + widened(back_a)
    s2 = near_sums[2 * n :] + widened(z1(rounded(s3)))
    quad_sums = image_part(f32, w_aq, *late(0, s2))
    s01 = near_sums[: 2 * n] + widened(z2(rounded(s2)))
    quad_sums = quad_sums + widened(back_d) + widened(back_x) + widened(back_y)
    text_grad = grad_rows(coefficients, texts, images, s01[:n], z1(rounded(s01[n:])))
    image_grad = grad_rows(
        coefficients,
        images,
        texts,
        quad_sums[:n],
        d1(rounded(quad_sums[3 * n :])),
        x1(rounded(quad_sums[n : 2 * n])),
        y1(rounded(quad_sums[2 * n : 3 * n])),
    )
    return (image_grad, text_grad)


def solution(mesh):
    in_specs = (P(AXES, None), P(AXES, None), P(), P())
    out_specs = (P(AXES, None), P(AXES, None))
    return jax.shard_map(local, mesh=mesh, in_specs=in_specs, out_specs=out_specs, check_vma=False)
```

```python
import functools

import jax
import jax.numpy as jnp
from jax import lax
from jax.experimental import pallas as pl
from jax.experimental.pallas import tpu as pltpu
from jax.sharding import PartitionSpec as P

epsilon = 1e-06
log2_e = 1.4426950408889634
AXES = ("blk", "grp")


def place(x, y, z, core):
    return ((((y >> 1) * 8 + z) * 2 + core) * 2 + (y & 1)) * 4 + x


def partner(position, size, first):
    step = 1 if (position % 2 == 0) == first else -1
    return (position + step) % size


def pairs_of(axis, first):
    pairs = []
    for x in range(4):
        for y in range(4):
            for z in range(8):
                for core in range(2):
                    side = first == (core == 0)
                    to = [x, y, z, core]
                    if axis == "x":
                        to[0] = partner(x, 4, side)
                    elif axis == "y":
                        to[1] = partner(y, 4, side)
                    elif axis == "z":
                        to[2] = partner(z, 8, side)
                    else:
                        to[3] = 1 - core
                    pairs.append((place(x, y, z, core), place(*to)))
    return sorted(pairs)


def permute(*hops):
    maps = [dict(pairs_of(axis, first)) for axis, first in hops]
    pairs = []
    for source in sorted(maps[0]):
        target = source
        for hop in maps:
            target = hop[target]
        pairs.append((source, target))
    return lambda value: lax.ppermute(value, AXES, pairs)


def unit_rows(values):
    widened = values.astype(jnp.float32)
    inverse = lax.rsqrt(jnp.sum(widened * widened, axis=1, keepdims=True) + epsilon)
    return (widened * inverse, inverse)


def through_norm(unit_part, inverse, along_unit):
    projected = jnp.sum(unit_part * along_unit, axis=1, keepdims=True)
    return (along_unit - unit_part * projected) * inverse


def rounded(value):
    return value.astype(jnp.bfloat16)


def widened(value):
    return value.astype(jnp.float32)


def join(*parts):
    return jnp.concatenate(parts, axis=0)


def unit_kernel(rows, units):
    units[...] = rounded(unit_rows(rows[...])[0])


def block_kernel(own, *refs):
    *arrived, block = refs
    n = own.shape[0]
    block[pl.ds(0, n)] = own[...]
    for index, rows in enumerate(arrived):
        block[pl.ds((index + 1) * n, n)] = rounded(unit_rows(rows[...])[0])


def grad_kernel(coefficients, rows, others, sums, *rest):
    *arrived, grad = rest
    unit, inverse = unit_rows(rows[...])
    other_send = widened(rounded(unit_rows(others[...])[0]))
    total = sums[...] - scale_and_bias(coefficients)[0] * other_send
    for part in arrived:
        total = total + widened(part[...])
    grad[...] = through_norm(unit, inverse, total)


def grad_rows(coefficients, rows, others, sums, *arrived):
    whole = pl.BlockSpec(memory_space=pltpu.VMEM)
    return pl.pallas_call(
        grad_kernel,
        out_shape=jax.ShapeDtypeStruct(rows.shape, jnp.float32),
        in_specs=[whole] * (4 + len(arrived)),
        out_specs=whole,
        compiler_params=pltpu.CompilerParams(vmem_limit_bytes=4 * 2**20),
    )(coefficients, rows, others, sums, *arrived)


def weights_of(factor, offset, texts, images):
    logits = lax.dot_general(
        texts[...], images[...], (((1,), (1,)), ((), ())), preferred_element_type=jnp.float32
    )
    decay = jnp.exp2(logits * (factor * -log2_e) + offset * -log2_e)
    return rounded(factor / (1.0 + decay))


def for_images(weights, texts):
    return lax.dot_general(
        weights, texts[...], (((0,), (0,)), ((), ())), preferred_element_type=jnp.float32
    )


def for_texts(weights, images):
    return jnp.dot(weights, images[...], preferred_element_type=jnp.float32)


def scale_and_bias(coefficients):
    return coefficients[0:1, 0:1], coefficients[4:5, 0:1]


def rows_of(*refs):
    return jnp.concatenate([ref[...] for ref in refs], axis=0)


def columns_of(*parts):
    return jnp.concatenate(parts, axis=1)


def weight_kernel(count, coefficients, *refs):
    *inputs, weights = refs
    weights[...] = weights_of(
        *scale_and_bias(coefficients), rows_of(*inputs[:count]), rows_of(*inputs[count:])
    )


def part_kernel(w_aq, w_axy, quad, part_x, part_y, sums):
    sums[...] = for_texts(columns_of(w_aq[...], w_axy[...]), rows_of(quad, part_x, part_y))


def near_kernel(part, w_ad, top_d, low_d, sums_own, send):
    total = part[...] + for_texts(w_ad[...], rows_of(top_d, low_d))
    own = sums_own.shape[0]
    sums_own[...] = total[:own]
    send[...] = rounded(total[own:])


def sibling_kernel(coefficients, sib_c, quad, part_x, part_y, top_d, low_d, weights, send):
    images = rows_of(quad, part_x, part_y, top_d, low_d)
    weights[...] = weights_of(*scale_and_bias(coefficients), sib_c, images)
    send[...] = rounded(for_texts(weights[...], images))


def text_kernel(weights, *refs):
    *images, sums = refs
    sums[...] = for_texts(weights[...], rows_of(*images))


def image_kernel(count, *refs):
    *inputs, sums = refs
    total = for_images(rows_of(*inputs[:count]), rows_of(*inputs[count:]))
    sums[...] = total.astype(sums.dtype)


def on_device(kernel, outputs, *operands, products=0):
    vmem = pl.BlockSpec(memory_space=pltpu.VMEM)
    width = operands[-1].shape[-1]
    return pl.pallas_call(
        kernel,
        out_shape=[jax.ShapeDtypeStruct(shape, kind) for shape, kind in outputs],
        in_specs=[vmem] * len(operands),
        out_specs=[vmem] * len(outputs),
        compiler_params=pltpu.CompilerParams(vmem_limit_bytes=16 * 2**20),
        cost_estimate=pl.CostEstimate(
            flops=2 * width * products, bytes_accessed=0, transcendentals=0
        ),
    )(*operands)


def after(value, *others):
    return lax.optimization_barrier((value,) + others)[0]


def local(images, texts, logit_scale, logit_bias):
    x1, y1, d1 = permute(("x", True)), permute(("y", True)), permute(("x", True), ("y", True))
    x2, y2, d2 = permute(("x", False)), permute(("y", False)), permute(("x", False), ("y", False))
    z1, z2 = permute(("z", True)), permute(("z", False))
    z_out, z_home = permute(("z", True), ("z", False)), permute(("z", False), ("z", True))
    sibling = permute(("core", True))
    f32, bf16 = jnp.float32, jnp.bfloat16
    n, d = images.shape
    a, b, q = 4 * n, 2 * n, 4 * n
    coefficients = join(*[jnp.broadcast_to(v, (4, 128)) for v in (logit_scale, logit_bias)])
    coefficients = join(*[jnp.broadcast_to(v, (4, 128)) for v in (logit_scale, logit_bias)])

    def units_of(rows):
        return on_device(unit_kernel, [((n, d), bf16)], rows)[0]

    def block_of(own, *arrived):
        return on_device(block_kernel, [(((1 + len(arrived)) * n, d), bf16)], own, *arrived)[0]

    def weigh(some_texts, some_images, share=1):
        m = sum(v.shape[0] for v in some_texts)
        k = sum(v.shape[0] for v in some_images)
        return on_device(
            functools.partial(weight_kernel, len(some_texts)), [((m, k), bf16)],
            coefficients, *some_texts, *some_images, products=share * m * k,
        )[0]

    raw = (z1(texts), y1(images), x1(images), d1(images), units_of(texts), units_of(images), coefficients)
    raw_t, raw_y, raw_x, raw_d, own_text, own_image, coefficients = lax.optimization_barrier(raw)
    pair = block_of(own_text, raw_t)
    quad = block_of(own_image, raw_x, raw_y, raw_d)
    r2 = z2(pair)
    part_x, part_y = x2(quad), y2(quad)
    r3, r4 = z1(r2), z_out(r2)
    top_d, low_d = y2(part_x[: q // 2]), x2(part_y[q // 2 :])
    own_a = join(pair, r2)
    sib_a = sibling(own_a)
    w_aq = weigh((own_a, sib_a), (quad,), share=0)
    w_axy = weigh((own_a, sib_a), (part_x, part_y), share=0)
    w_ad = weigh((after(own_a, w_aq, w_axy), sib_a), (top_d, low_d))
    all_images = (quad, part_x, part_y, top_d, low_d)

    (near_part,) = on_device(part_kernel, [((2 * a, d), f32)], w_aq, w_axy, quad, part_x, part_y)
    r3, r4, w_aq, w_axy, near_part = lax.optimization_barrier((r3, r4, w_aq, w_axy, near_part))
    own_c = join(r3, r4)
    sib_c = sibling(own_c)
    w_own = weigh((own_c,), all_images)
    w_sib, send_c = on_device(
        sibling_kernel, [((a, 4 * q), bf16), ((a, d), bf16)], coefficients, sib_c, *all_images,
        products=2 * a * 4 * q,
    )
    (sums_own_c,) = on_device(
        text_kernel, [((a, d), f32)], w_own, *all_images, products=a * 4 * q
    )
    back_c = sibling(send_c)
    all_texts = (own_a, sib_a, own_c, sib_c)

    def image_part(kind, *blocks, share=1):
        return on_device(
            functools.partial(image_kernel, len(blocks)), [((q, d), kind)],
            *blocks, *all_texts, products=share * q * 4 * q,
        )[0]

    def late(index, *others):
        span = slice(index * q, (index + 1) * q)
        return after(w_own[:, span], *others), w_sib[:, span]

    send_d = image_part(bf16, w_ad, *late(3))
    back_d = d2(send_d)
    s4 = rounded(after(sums_own_c, send_d) + widened(back_c))
    send_x = image_part(bf16, w_axy[:, :q], *late(1, s4))
    send_y = image_part(bf16, w_axy[:, q:], *late(2, s4))
    back_x, back_y = x2(send_x), y2(send_y)
    sums_own, send_a = on_device(
        near_kernel, [((a, d), f32), ((a, d), bf16)], near_part, after(w_ad, s4), top_d, low_d,
        products=2 * a * 4 * q,
    )
    back_a = sibling(send_a)
    back_3, back_4 = z1(s4[:b]), z_home(s4[b:])
    near_sums = sums_own + widened(back_a)
    s2 = near_sums[2 * n :] + widened(back_3) + widened(back_4)
    quad_sums = image_part(f32, w_aq, *late(0, s2))
    s01 = near_sums[: 2 * n] + widened(z2(rounded(s2)))
    quad_sums = quad_sums + widened(back_d) + widened(back_x) + widened(back_y)
    text_grad = grad_rows(coefficients, texts, images, s01[:n], z1(rounded(s01[n:])))
    image_grad = grad_rows(
        coefficients,
        images,
        texts,
        quad_sums[:n],
        d1(rounded(quad_sums[3 * n :])),
        x1(rounded(quad_sums[n : 2 * n])),
        y1(rounded(quad_sums[2 * n : 3 * n])),
    )
    return (image_grad, text_grad)


def solution(mesh):
    in_specs = (P(AXES, None), P(AXES, None), P(), P())
    out_specs = (P(AXES, None), P(AXES, None))
    return jax.shard_map(local, mesh=mesh, in_specs=in_specs, out_specs=out_specs, check_vma=False)
```

```python
import functools

import jax
import jax.numpy as jnp
from jax import lax
from jax.experimental import pallas as pl
from jax.experimental.pallas import tpu as pltpu
from jax.sharding import PartitionSpec as P

epsilon = 1e-06
log2_e = 1.4426950408889634
AXES = ("blk", "grp")


def place(x, y, z, core):
    return ((((y >> 1) * 8 + z) * 2 + core) * 2 + (y & 1)) * 4 + x


def partner(position, size, first):
    step = 1 if (position % 2 == 0) == first else -1
    return (position + step) % size


def pairs_of(axis, first):
    pairs = []
    for x in range(4):
        for y in range(4):
            for z in range(8):
                for core in range(2):
                    side = first == (core == (1 if axis == "z" else 0))
                    to = [x, y, z, core]
                    if axis == "x":
                        to[0] = partner(x, 4, side)
                    elif axis == "y":
                        to[1] = partner(y, 4, side)
                    elif axis == "z":
                        to[2] = partner(z, 8, side)
                    else:
                        to[3] = 1 - core
                    pairs.append((place(x, y, z, core), place(*to)))
    return sorted(pairs)


def permute(*hops):
    maps = [dict(pairs_of(axis, first)) for axis, first in hops]
    pairs = []
    for source in sorted(maps[0]):
        target = source
        for hop in maps:
            target = hop[target]
        pairs.append((source, target))
    return lambda value: lax.ppermute(value, AXES, pairs)


def unit_rows(values):
    widened = values.astype(jnp.float32)
    inverse = lax.rsqrt(jnp.sum(widened * widened, axis=1, keepdims=True) + epsilon)
    return (widened * inverse, inverse)


def through_norm(unit_part, inverse, along_unit):
    projected = jnp.sum(unit_part * along_unit, axis=1, keepdims=True)
    return (along_unit - unit_part * projected) * inverse


def rounded(value):
    return value.astype(jnp.bfloat16)


def widened(value):
    return value.astype(jnp.float32)


def join(*parts):
    return jnp.concatenate(parts, axis=0)


def unit_kernel(rows, units):
    units[...] = rounded(unit_rows(rows[...])[0])


def block_kernel(own, *refs):
    *arrived, block = refs
    n = own.shape[0]
    block[pl.ds(0, n)] = own[...]
    for index, rows in enumerate(arrived):
        block[pl.ds((index + 1) * n, n)] = rounded(unit_rows(rows[...])[0])


def grad_kernel(coefficients, rows, others, sums, *rest):
    *arrived, grad = rest
    unit, inverse = unit_rows(rows[...])
    other_send = widened(rounded(unit_rows(others[...])[0]))
    total = sums[...] - scale_and_bias(coefficients)[0] * other_send
    for part in arrived:
        total = total + widened(part[...])
    grad[...] = through_norm(unit, inverse, total)


def grad_rows(coefficients, rows, others, sums, *arrived):
    whole = pl.BlockSpec(memory_space=pltpu.VMEM)
    return pl.pallas_call(
        grad_kernel,
        out_shape=jax.ShapeDtypeStruct(rows.shape, jnp.float32),
        in_specs=[whole] * (4 + len(arrived)),
        out_specs=whole,
        compiler_params=pltpu.CompilerParams(vmem_limit_bytes=4 * 2**20),
    )(coefficients, rows, others, sums, *arrived)


def weights_of(factor, offset, texts, images):
    logits = lax.dot_general(
        texts[...], images[...], (((1,), (1,)), ((), ())), preferred_element_type=jnp.float32
    )
    decay = jnp.exp2(logits * (factor * -log2_e) + offset * -log2_e)
    return rounded(factor / (1.0 + decay))


def for_images(weights, texts):
    return lax.dot_general(
        weights, texts[...], (((0,), (0,)), ((), ())), preferred_element_type=jnp.float32
    )


def for_texts(weights, images):
    return jnp.dot(weights, images[...], preferred_element_type=jnp.float32)


def scale_and_bias(coefficients):
    return coefficients[0:1, 0:1], coefficients[4:5, 0:1]


def rows_of(*refs):
    return jnp.concatenate([ref[...] for ref in refs], axis=0)


def columns_of(*parts):
    return jnp.concatenate(parts, axis=1)


def weight_kernel(count, coefficients, *refs):
    *inputs, weights = refs
    weights[...] = weights_of(
        *scale_and_bias(coefficients), rows_of(*inputs[:count]), rows_of(*inputs[count:])
    )


def part_kernel(w_aq, w_axy, quad, part_x, part_y, sums):
    sums[...] = for_texts(columns_of(w_aq[...], w_axy[...]), rows_of(quad, part_x, part_y))


def near_kernel(part, w_ad, top_d, low_d, sums_own, send):
    total = part[...] + for_texts(w_ad[...], rows_of(top_d, low_d))
    own = sums_own.shape[0]
    sums_own[...] = total[:own]
    send[...] = rounded(total[own:])


def sibling_kernel(coefficients, sib_c, quad, part_x, part_y, top_d, low_d, weights, send):
    images = rows_of(quad, part_x, part_y, top_d, low_d)
    weights[...] = weights_of(*scale_and_bias(coefficients), sib_c, images)
    send[...] = rounded(for_texts(weights[...], images))


def text_kernel(weights, *refs):
    *images, sums = refs
    sums[...] = for_texts(weights[...], rows_of(*images))


def image_kernel(count, *refs):
    *inputs, sums = refs
    total = for_images(rows_of(*inputs[:count]), rows_of(*inputs[count:]))
    sums[...] = total.astype(sums.dtype)


def on_device(kernel, outputs, *operands, products=0):
    vmem = pl.BlockSpec(memory_space=pltpu.VMEM)
    width = operands[-1].shape[-1]
    return pl.pallas_call(
        kernel,
        out_shape=[jax.ShapeDtypeStruct(shape, kind) for shape, kind in outputs],
        in_specs=[vmem] * len(operands),
        out_specs=[vmem] * len(outputs),
        compiler_params=pltpu.CompilerParams(vmem_limit_bytes=16 * 2**20),
        cost_estimate=pl.CostEstimate(
            flops=2 * width * products, bytes_accessed=0, transcendentals=0
        ),
    )(*operands)


def after(value, *others):
    return lax.optimization_barrier((value,) + others)[0]


def local(images, texts, logit_scale, logit_bias):
    x1, y1, d1 = permute(("x", True)), permute(("y", True)), permute(("x", True), ("y", True))
    x2, y2, d2 = permute(("x", False)), permute(("y", False)), permute(("x", False), ("y", False))
    z1, z2 = permute(("z", True)), permute(("z", False))
    z_out, z_home = permute(("z", True), ("z", False)), permute(("z", False), ("z", True))
    sibling = permute(("core", True))
    f32, bf16 = jnp.float32, jnp.bfloat16
    n, d = images.shape
    a, b, q = 4 * n, 2 * n, 4 * n
    coefficients = join(*[jnp.broadcast_to(v, (4, 128)) for v in (logit_scale, logit_bias)])
    coefficients = join(*[jnp.broadcast_to(v, (4, 128)) for v in (logit_scale, logit_bias)])

    def units_of(rows):
        return on_device(unit_kernel, [((n, d), bf16)], rows)[0]

    def block_of(own, *arrived):
        return on_device(block_kernel, [(((1 + len(arrived)) * n, d), bf16)], own, *arrived)[0]

    def weigh(some_texts, some_images, share=1):
        m = sum(v.shape[0] for v in some_texts)
        k = sum(v.shape[0] for v in some_images)
        return on_device(
            functools.partial(weight_kernel, len(some_texts)), [((m, k), bf16)],
            coefficients, *some_texts, *some_images, products=share * m * k,
        )[0]

    raw = (z1(texts), y1(images), x1(images), d1(images), units_of(texts), units_of(images), coefficients)
    raw_t, raw_y, raw_x, raw_d, own_text, own_image, coefficients = lax.optimization_barrier(raw)
    pair = block_of(own_text, raw_t)
    quad = block_of(own_image, raw_x, raw_y, raw_d)
    r2 = z2(pair)
    part_x, part_y = x2(quad), y2(quad)
    r3, r4 = z1(r2), z_out(r2)
    top_d, low_d = y2(part_x[: q // 2]), x2(part_y[q // 2 :])
    own_a = join(pair, r2)
    sib_a = sibling(own_a)
    w_aq = weigh((own_a, sib_a), (quad,), share=0)
    w_axy = weigh((own_a, sib_a), (part_x, part_y), share=0)
    w_ad = weigh((after(own_a, w_aq, w_axy), sib_a), (top_d, low_d))
    all_images = (quad, part_x, part_y, top_d, low_d)

    (near_part,) = on_device(part_kernel, [((2 * a, d), f32)], w_aq, w_axy, quad, part_x, part_y)
    r3, r4, w_aq, w_axy, near_part = lax.optimization_barrier((r3, r4, w_aq, w_axy, near_part))
    own_c = join(r3, r4)
    sib_c = sibling(own_c)
    w_own = weigh((own_c,), all_images)
    w_sib, send_c = on_device(
        sibling_kernel, [((a, 4 * q), bf16), ((a, d), bf16)], coefficients, sib_c, *all_images,
        products=2 * a * 4 * q,
    )
    (sums_own_c,) = on_device(
        text_kernel, [((a, d), f32)], w_own, *all_images, products=a * 4 * q
    )
    back_c = sibling(send_c)
    all_texts = (own_a, sib_a, own_c, sib_c)

    def image_part(kind, *blocks, share=1):
        return on_device(
            functools.partial(image_kernel, len(blocks)), [((q, d), kind)],
            *blocks, *all_texts, products=share * q * 4 * q,
        )[0]

    def late(index, *others):
        span = slice(index * q, (index + 1) * q)
        return after(w_own[:, span], *others), w_sib[:, span]

    send_d = image_part(bf16, w_ad, *late(3))
    back_d = d2(send_d)
    s4 = rounded(after(sums_own_c, send_d) + widened(back_c))
    send_x = image_part(bf16, w_axy[:, :q], *late(1, s4))
    send_y = image_part(bf16, w_axy[:, q:], *late(2, s4))
    back_x, back_y = x2(send_x), y2(send_y)
    sums_own, send_a = on_device(
        near_kernel, [((a, d), f32), ((a, d), bf16)], near_part, after(w_ad, s4), top_d, low_d,
        products=2 * a * 4 * q,
    )
    back_a = sibling(send_a)
    back_3, back_4 = z1(s4[:b]), z_home(s4[b:])
    near_sums = sums_own + widened(back_a)
    s2 = near_sums[2 * n :] + widened(back_3) + widened(back_4)
    quad_sums = image_part(f32, w_aq, *late(0, s2))
    s01 = near_sums[: 2 * n] + widened(z2(rounded(s2)))
    quad_sums = quad_sums + widened(back_d) + widened(back_x) + widened(back_y)
    text_grad = grad_rows(coefficients, texts, images, s01[:n], z1(rounded(s01[n:])))
    image_grad = grad_rows(
        coefficients,
        images,
        texts,
        quad_sums[:n],
        y1(rounded(quad_sums[2 * n : 3 * n])),
        x1(rounded(quad_sums[n : 2 * n])),
        d1(rounded(quad_sums[3 * n :])),
    )
    return (image_grad, text_grad)


def solution(mesh):
    in_specs = (P(AXES, None), P(AXES, None), P(), P())
    out_specs = (P(AXES, None), P(AXES, None))
    return jax.shard_map(local, mesh=mesh, in_specs=in_specs, out_specs=out_specs, check_vma=False)
```

```python
import functools

import jax
import jax.numpy as jnp
from jax import lax
from jax.experimental import pallas as pl
from jax.experimental.pallas import tpu as pltpu
from jax.sharding import PartitionSpec as P

epsilon = 1e-06
log2_e = 1.4426950408889634
AXES = ("blk", "grp")


def place(x, y, z, core):
    return ((((y >> 1) * 8 + z) * 2 + core) * 2 + (y & 1)) * 4 + x


def partner(position, size, first):
    step = 1 if (position % 2 == 0) == first else -1
    return (position + step) % size


def pairs_of(axis, first):
    pairs = []
    for x in range(4):
        for y in range(4):
            for z in range(8):
                for core in range(2):
                    side = first == (core == (1 if axis == "z" else 0))
                    to = [x, y, z, core]
                    if axis == "x":
                        to[0] = partner(x, 4, side)
                    elif axis == "y":
                        to[1] = partner(y, 4, side)
                    elif axis == "z":
                        to[2] = partner(z, 8, side)
                    else:
                        to[3] = 1 - core
                    pairs.append((place(x, y, z, core), place(*to)))
    return sorted(pairs)


def permute(*hops):
    maps = [dict(pairs_of(axis, first)) for axis, first in hops]
    pairs = []
    for source in sorted(maps[0]):
        target = source
        for hop in maps:
            target = hop[target]
        pairs.append((source, target))
    return lambda value: lax.ppermute(value, AXES, pairs)


def unit_rows(values):
    widened = values.astype(jnp.float32)
    inverse = lax.rsqrt(jnp.sum(widened * widened, axis=1, keepdims=True) + epsilon)
    return (widened * inverse, inverse)


def through_norm(unit_part, inverse, along_unit):
    projected = jnp.sum(unit_part * along_unit, axis=1, keepdims=True)
    return (along_unit - unit_part * projected) * inverse


def rounded(value):
    return value.astype(jnp.bfloat16)


def widened(value):
    return value.astype(jnp.float32)


def join(*parts):
    return jnp.concatenate(parts, axis=0)


def unit_kernel(rows, units):
    units[...] = rounded(unit_rows(rows[...])[0])


def block_kernel(own, *refs):
    *arrived, block = refs
    n = own.shape[0]
    block[pl.ds(0, n)] = own[...]
    for index, rows in enumerate(arrived):
        block[pl.ds((index + 1) * n, n)] = rounded(unit_rows(rows[...])[0])


def grad_kernel(coefficients, rows, others, sums, *rest):
    *arrived, grad, held, sent = rest
    half = held.shape[0] // 2
    copies = []
    for index in range(2):
        span = pl.ds(index * half, half)
        unit, inverse = unit_rows(rows[span])
        other_send = widened(rounded(unit_rows(others[span])[0]))
        total = sums[span] - scale_and_bias(coefficients)[0] * other_send
        for part in arrived:
            total = total + widened(part[span])
        held[span] = through_norm(unit, inverse, total)
        copies.append(pltpu.make_async_copy(held.at[span], grad.at[span], sent.at[index]))
        copies[-1].start()
    for copy in copies:
        copy.wait()


def grad_rows(coefficients, rows, others, sums, *arrived):
    whole = pl.BlockSpec(memory_space=pltpu.VMEM)
    return pl.pallas_call(
        grad_kernel,
        out_shape=jax.ShapeDtypeStruct(rows.shape, jnp.float32),
        in_specs=[whole] * (4 + len(arrived)),
        out_specs=pl.BlockSpec(memory_space=pl.ANY),
        scratch_shapes=[pltpu.VMEM(rows.shape, jnp.float32), pltpu.SemaphoreType.DMA((2,))],
        compiler_params=pltpu.CompilerParams(vmem_limit_bytes=4 * 2**20),
    )(coefficients, rows, others, sums, *arrived)


def weights_of(factor, offset, texts, images):
    logits = lax.dot_general(
        texts[...], images[...], (((1,), (1,)), ((), ())), preferred_element_type=jnp.float32
    )
    decay = jnp.exp2(logits * (factor * -log2_e) + offset * -log2_e)
    return rounded(factor / (1.0 + decay))


def for_images(weights, texts):
    return lax.dot_general(
        weights, texts[...], (((0,), (0,)), ((), ())), preferred_element_type=jnp.float32
    )


def for_texts(weights, images):
    return jnp.dot(weights, images[...], preferred_element_type=jnp.float32)


def scale_and_bias(coefficients):
    return coefficients[0:1, 0:1], coefficients[4:5, 0:1]


def rows_of(*refs):
    return jnp.concatenate([ref[...] for ref in refs], axis=0)


def columns_of(*parts):
    return jnp.concatenate(parts, axis=1)


def weight_kernel(count, coefficients, *refs):
    *inputs, weights = refs
    weights[...] = weights_of(
        *scale_and_bias(coefficients), rows_of(*inputs[:count]), rows_of(*inputs[count:])
    )


def part_kernel(w_aq, w_axy, quad, part_x, part_y, sums):
    sums[...] = for_texts(columns_of(w_aq[...], w_axy[...]), rows_of(quad, part_x, part_y))


def near_kernel(part, w_ad, top_d, low_d, sums_own, send):
    total = part[...] + for_texts(w_ad[...], rows_of(top_d, low_d))
    own = sums_own.shape[0]
    sums_own[...] = total[:own]
    send[...] = rounded(total[own:])


def sibling_kernel(coefficients, sib_c, quad, part_x, part_y, top_d, low_d, weights, send):
    images = rows_of(quad, part_x, part_y, top_d, low_d)
    weights[...] = weights_of(*scale_and_bias(coefficients), sib_c, images)
    send[...] = rounded(for_texts(weights[...], images))


def text_kernel(weights, *refs):
    *images, sums = refs
    sums[...] = for_texts(weights[...], rows_of(*images))


def image_kernel(count, *refs):
    *inputs, sums = refs
    total = for_images(rows_of(*inputs[:count]), rows_of(*inputs[count:]))
    sums[...] = total.astype(sums.dtype)


def on_device(kernel, outputs, *operands, products=0):
    vmem = pl.BlockSpec(memory_space=pltpu.VMEM)
    width = operands[-1].shape[-1]
    return pl.pallas_call(
        kernel,
        out_shape=[jax.ShapeDtypeStruct(shape, kind) for shape, kind in outputs],
        in_specs=[vmem] * len(operands),
        out_specs=[vmem] * len(outputs),
        compiler_params=pltpu.CompilerParams(vmem_limit_bytes=16 * 2**20),
        cost_estimate=pl.CostEstimate(
            flops=2 * width * products, bytes_accessed=0, transcendentals=0
        ),
    )(*operands)


def after(value, *others):
    return lax.optimization_barrier((value,) + others)[0]


def local(images, texts, logit_scale, logit_bias):
    x1, y1, d1 = permute(("x", True)), permute(("y", True)), permute(("x", True), ("y", True))
    x2, y2, d2 = permute(("x", False)), permute(("y", False)), permute(("x", False), ("y", False))
    z1, z2 = permute(("z", True)), permute(("z", False))
    z_out, z_home = permute(("z", True), ("z", False)), permute(("z", False), ("z", True))
    sibling = permute(("core", True))
    f32, bf16 = jnp.float32, jnp.bfloat16
    n, d = images.shape
    a, b, q = 4 * n, 2 * n, 4 * n
    coefficients = join(*[jnp.broadcast_to(v, (4, 128)) for v in (logit_scale, logit_bias)])
    coefficients = join(*[jnp.broadcast_to(v, (4, 128)) for v in (logit_scale, logit_bias)])

    def units_of(rows):
        return on_device(unit_kernel, [((n, d), bf16)], rows)[0]

    def block_of(own, *arrived):
        return on_device(block_kernel, [(((1 + len(arrived)) * n, d), bf16)], own, *arrived)[0]

    def weigh(some_texts, some_images, share=1):
        m = sum(v.shape[0] for v in some_texts)
        k = sum(v.shape[0] for v in some_images)
        return on_device(
            functools.partial(weight_kernel, len(some_texts)), [((m, k), bf16)],
            coefficients, *some_texts, *some_images, products=share * m * k,
        )[0]

    raw = (z1(texts), y1(images), x1(images), d1(images), units_of(texts), units_of(images), coefficients)
    raw_t, raw_y, raw_x, raw_d, own_text, own_image, coefficients = lax.optimization_barrier(raw)
    pair = block_of(own_text, raw_t)
    quad = block_of(own_image, raw_x, raw_y, raw_d)
    r2 = z2(pair)
    part_x, part_y = x2(quad), y2(quad)
    r3, r4 = z1(r2), z_out(r2)
    top_d, low_d = y2(part_x[: q // 2]), x2(part_y[q // 2 :])
    own_a = join(pair, r2)
    sib_a = sibling(own_a)
    w_aq = weigh((own_a, sib_a), (quad,), share=0)
    w_axy = weigh((own_a, sib_a), (part_x, part_y), share=0)
    w_ad = weigh((after(own_a, w_aq, w_axy), sib_a), (top_d, low_d))
    all_images = (quad, part_x, part_y, top_d, low_d)

    (near_part,) = on_device(part_kernel, [((2 * a, d), f32)], w_aq, w_axy, quad, part_x, part_y)
    r3, r4, w_aq, w_axy, near_part = lax.optimization_barrier((r3, r4, w_aq, w_axy, near_part))
    own_c = join(r3, r4)
    sib_c = sibling(own_c)
    w_own = weigh((own_c,), all_images)
    w_sib, send_c = on_device(
        sibling_kernel, [((a, 4 * q), bf16), ((a, d), bf16)], coefficients, sib_c, *all_images,
        products=2 * a * 4 * q,
    )
    (sums_own_c,) = on_device(
        text_kernel, [((a, d), f32)], w_own, *all_images, products=a * 4 * q
    )
    back_c = sibling(send_c)
    all_texts = (own_a, sib_a, own_c, sib_c)

    def image_part(kind, *blocks, share=1):
        return on_device(
            functools.partial(image_kernel, len(blocks)), [((q, d), kind)],
            *blocks, *all_texts, products=share * q * 4 * q,
        )[0]

    def late(index, *others):
        span = slice(index * q, (index + 1) * q)
        return after(w_own[:, span], *others), w_sib[:, span]

    send_d = image_part(bf16, w_ad, *late(3))
    back_d = d2(send_d)
    s4 = rounded(after(sums_own_c, send_d) + widened(back_c))
    send_x = image_part(bf16, w_axy[:, :q], *late(1, s4))
    send_y = image_part(bf16, w_axy[:, q:], *late(2, s4))
    back_x, back_y = x2(send_x), y2(send_y)
    sums_own, send_a = on_device(
        near_kernel, [((a, d), f32), ((a, d), bf16)], near_part, after(w_ad, s4), top_d, low_d,
        products=2 * a * 4 * q,
    )
    back_a = sibling(send_a)
    back_3, back_4 = z1(s4[:b]), z_home(s4[b:])
    near_sums = sums_own + widened(back_a)
    s2 = near_sums[2 * n :] + widened(back_3) + widened(back_4)
    quad_sums = image_part(f32, w_aq, *late(0, s2))
    s01 = near_sums[: 2 * n] + widened(z2(rounded(s2)))
    quad_sums = quad_sums + widened(back_d) + widened(back_x) + widened(back_y)
    text_grad = grad_rows(coefficients, texts, images, s01[:n], z1(rounded(s01[n:])))
    image_grad = grad_rows(
        coefficients,
        images,
        texts,
        quad_sums[:n],
        y1(rounded(quad_sums[2 * n : 3 * n])),
        x1(rounded(quad_sums[n : 2 * n])),
        d1(rounded(quad_sums[3 * n :])),
    )
    return (image_grad, text_grad)


def solution(mesh):
    in_specs = (P(AXES, None), P(AXES, None), P(), P())
    out_specs = (P(AXES, None), P(AXES, None))
    return jax.shard_map(local, mesh=mesh, in_specs=in_specs, out_specs=out_specs, check_vma=False)
```

```python
import functools

import jax
import jax.numpy as jnp
from jax import lax
from jax.experimental import pallas as pl
from jax.experimental.pallas import tpu as pltpu
from jax.sharding import PartitionSpec as P

epsilon = 1e-06
log2_e = 1.4426950408889634
AXES = ("blk", "grp")


def place(x, y, z, core):
    return ((((y >> 1) * 8 + z) * 2 + core) * 2 + (y & 1)) * 4 + x


def partner(position, size, first):
    step = 1 if (position % 2 == 0) == first else -1
    return (position + step) % size


def pairs_of(axis, first):
    pairs = []
    for x in range(4):
        for y in range(4):
            for z in range(8):
                for core in range(2):
                    side = first == (core == (1 if axis == "z" else 0))
                    to = [x, y, z, core]
                    if axis == "x":
                        to[0] = partner(x, 4, side)
                    elif axis == "y":
                        to[1] = partner(y, 4, side)
                    elif axis == "z":
                        to[2] = partner(z, 8, side)
                    else:
                        to[3] = 1 - core
                    pairs.append((place(x, y, z, core), place(*to)))
    return sorted(pairs)


def permute(*hops):
    maps = [dict(pairs_of(axis, first)) for axis, first in hops]
    pairs = []
    for source in sorted(maps[0]):
        target = source
        for hop in maps:
            target = hop[target]
        pairs.append((source, target))
    return lambda value: lax.ppermute(value, AXES, pairs)


def unit_rows(values):
    widened = values.astype(jnp.float32)
    inverse = lax.rsqrt(jnp.sum(widened * widened, axis=1, keepdims=True) + epsilon)
    return (widened * inverse, inverse)


def through_norm(unit_part, inverse, along_unit):
    projected = jnp.sum(unit_part * along_unit, axis=1, keepdims=True)
    return (along_unit - unit_part * projected) * inverse


def rounded(value):
    return value.astype(jnp.bfloat16)


def widened(value):
    return value.astype(jnp.float32)


def join(*parts):
    return jnp.concatenate(parts, axis=0)


def unit_kernel(rows, units):
    units[...] = rounded(unit_rows(rows[...])[0])


def block_kernel(own, *refs):
    *arrived, block = refs
    n = own.shape[0]
    block[pl.ds(0, n)] = own[...]
    for index, rows in enumerate(arrived):
        block[pl.ds((index + 1) * n, n)] = rounded(unit_rows(rows[...])[0])


def grad_kernel(coefficients, rows, others, sums, *rest):
    *arrived, grad = rest
    unit, inverse = unit_rows(rows[...])
    other_send = widened(rounded(unit_rows(others[...])[0]))
    total = sums[...] - scale_and_bias(coefficients)[0] * other_send
    for part in arrived:
        total = total + widened(part[...])
    grad[...] = through_norm(unit, inverse, total)


def grad_rows(coefficients, rows, others, sums, *arrived):
    whole = pl.BlockSpec(memory_space=pltpu.VMEM)
    return pl.pallas_call(
        grad_kernel,
        out_shape=jax.ShapeDtypeStruct(rows.shape, jnp.float32),
        in_specs=[whole] * (4 + len(arrived)),
        out_specs=whole,
        compiler_params=pltpu.CompilerParams(vmem_limit_bytes=4 * 2**20),
    )(coefficients, rows, others, sums, *arrived)


def weights_of(factor, offset, texts, images):
    logits = lax.dot_general(
        texts[...], images[...], (((1,), (1,)), ((), ())), preferred_element_type=jnp.float32
    )
    decay = jnp.exp2(logits * (factor * -log2_e) + offset * -log2_e)
    return rounded(factor / (1.0 + decay))


def for_images(weights, texts):
    return lax.dot_general(
        weights, texts[...], (((0,), (0,)), ((), ())), preferred_element_type=jnp.float32
    )


def for_texts(weights, images):
    return jnp.dot(weights, images[...], preferred_element_type=jnp.float32)


def scale_and_bias(coefficients):
    return coefficients[0:1, 0:1], coefficients[4:5, 0:1]


def rows_of(*refs):
    return jnp.concatenate([ref[...] for ref in refs], axis=0)


def columns_of(*parts):
    return jnp.concatenate(parts, axis=1)


def weight_kernel(count, coefficients, *refs):
    *inputs, weights = refs
    weights[...] = weights_of(
        *scale_and_bias(coefficients), rows_of(*inputs[:count]), rows_of(*inputs[count:])
    )


def part_kernel(w_aq, w_axy, quad, part_x, part_y, sums):
    sums[...] = for_texts(columns_of(w_aq[...], w_axy[...]), rows_of(quad, part_x, part_y))


def near_kernel(part, w_ad, top_d, low_d, sums_own, send):
    total = part[...] + for_texts(w_ad[...], rows_of(top_d, low_d))
    own = sums_own.shape[0]
    sums_own[...] = total[:own]
    send[...] = rounded(total[own:])


def sibling_kernel(coefficients, sib_c, quad, part_x, part_y, top_d, low_d, weights, send):
    images = rows_of(quad, part_x, part_y, top_d, low_d)
    weights[...] = weights_of(*scale_and_bias(coefficients), sib_c, images)
    send[...] = rounded(for_texts(weights[...], images))


def text_kernel(weights, *refs):
    *images, sums = refs
    sums[...] = for_texts(weights[...], rows_of(*images))


def image_kernel(count, *refs):
    *inputs, sums = refs
    total = for_images(rows_of(*inputs[:count]), rows_of(*inputs[count:]))
    sums[...] = total.astype(sums.dtype)


def on_device(kernel, outputs, *operands, products=0):
    vmem = pl.BlockSpec(memory_space=pltpu.VMEM)
    width = operands[-1].shape[-1]
    return pl.pallas_call(
        kernel,
        out_shape=[jax.ShapeDtypeStruct(shape, kind) for shape, kind in outputs],
        in_specs=[vmem] * len(operands),
        out_specs=[vmem] * len(outputs),
        compiler_params=pltpu.CompilerParams(vmem_limit_bytes=16 * 2**20),
        cost_estimate=pl.CostEstimate(
            flops=2 * width * products, bytes_accessed=0, transcendentals=0
        ),
    )(*operands)


def after(value, *others):
    return lax.optimization_barrier((value,) + others)[0]


def local(images, texts, logit_scale, logit_bias):
    x1, y1, d1 = permute(("x", True)), permute(("y", True)), permute(("x", True), ("y", True))
    x2, y2, d2 = permute(("x", False)), permute(("y", False)), permute(("x", False), ("y", False))
    z1, z2 = permute(("z", True)), permute(("z", False))
    z_out, z_home = permute(("z", True), ("z", False)), permute(("z", False), ("z", True))
    sibling = permute(("core", True))
    f32, bf16 = jnp.float32, jnp.bfloat16
    n, d = images.shape
    a, b, q = 4 * n, 2 * n, 4 * n
    coefficients = join(*[jnp.broadcast_to(v, (4, 128)) for v in (logit_scale, logit_bias)])
    coefficients = join(*[jnp.broadcast_to(v, (4, 128)) for v in (logit_scale, logit_bias)])

    def units_of(rows):
        return on_device(unit_kernel, [((n, d), bf16)], rows)[0]

    def block_of(own, *arrived):
        return on_device(block_kernel, [(((1 + len(arrived)) * n, d), bf16)], own, *arrived)[0]

    def weigh(some_texts, some_images, share=1):
        m = sum(v.shape[0] for v in some_texts)
        k = sum(v.shape[0] for v in some_images)
        return on_device(
            functools.partial(weight_kernel, len(some_texts)), [((m, k), bf16)],
            coefficients, *some_texts, *some_images, products=share * m * k,
        )[0]

    raw = (z1(texts), y1(images), x1(images), d1(images), units_of(texts), units_of(images), coefficients)
    raw_t, raw_y, raw_x, raw_d, own_text, own_image, coefficients = lax.optimization_barrier(raw)
    pair = block_of(own_text, raw_t)
    quad = block_of(own_image, raw_x, raw_y, raw_d)
    r2 = z2(pair)
    part_x, part_y = x2(quad), y2(quad)
    r3, r4 = z1(r2), z_out(r2)
    top_d, low_d = y2(part_x[: q // 2]), x2(part_y[q // 2 :])
    own_a = join(pair, r2)
    sib_a = sibling(own_a)
    w_aq = weigh((own_a, sib_a), (quad,), share=0)
    w_axy = weigh((own_a, sib_a), (part_x, part_y), share=0)
    w_ad = weigh((after(own_a, w_aq, w_axy), sib_a), (top_d, low_d))
    all_images = (quad, part_x, part_y, top_d, low_d)

    (near_part,) = on_device(part_kernel, [((2 * a, d), f32)], w_aq, w_axy, quad, part_x, part_y)
    r3, r4, w_aq, w_axy, near_part = lax.optimization_barrier((r3, r4, w_aq, w_axy, near_part))
    own_c = join(r3, r4)
    sib_c = sibling(own_c)
    w_own = weigh((own_c,), all_images)
    w_sib, send_c = on_device(
        sibling_kernel, [((a, 4 * q), bf16), ((a, d), bf16)], coefficients, sib_c, *all_images,
        products=2 * a * 4 * q,
    )
    (sums_own_c,) = on_device(
        text_kernel, [((a, d), f32)], w_own, *all_images, products=a * 4 * q
    )
    back_c = sibling(send_c)
    all_texts = (own_a, sib_a, own_c, sib_c)

    def image_part(kind, *blocks, share=1):
        return on_device(
            functools.partial(image_kernel, len(blocks)), [((q, d), kind)],
            *blocks, *all_texts, products=share * q * 4 * q,
        )[0]

    def late(index, *others):
        span = slice(index * q, (index + 1) * q)
        return after(w_own[:, span], *others), w_sib[:, span]

    send_d = image_part(bf16, w_ad, *late(3))
    back_d = d2(send_d)
    s4 = rounded(sums_own_c + widened(back_c))
    send_x = image_part(bf16, w_axy[:, :q], *late(1, s4))
    send_y = image_part(bf16, w_axy[:, q:], *late(2, s4))
    back_x, back_y = x2(send_x), y2(send_y)
    sums_own, send_a = on_device(
        near_kernel, [((a, d), f32), ((a, d), bf16)], near_part, after(w_ad, s4), top_d, low_d,
        products=2 * a * 4 * q,
    )
    back_a = sibling(send_a)
    back_3, back_4 = z1(s4[:b]), z_home(s4[b:])
    near_sums = sums_own + widened(back_a)
    s2 = near_sums[2 * n :] + widened(back_3) + widened(back_4)
    quad_sums = image_part(f32, w_aq, *late(0, s2))
    s01 = near_sums[: 2 * n] + widened(z2(rounded(s2)))
    quad_sums = quad_sums + widened(back_d) + widened(back_x) + widened(back_y)
    text_grad = grad_rows(coefficients, texts, images, s01[:n], z1(rounded(s01[n:])))
    image_grad = grad_rows(
        coefficients,
        images,
        texts,
        quad_sums[:n],
        y1(rounded(quad_sums[2 * n : 3 * n])),
        x1(rounded(quad_sums[n : 2 * n])),
        d1(rounded(quad_sums[3 * n :])),
    )
    return (image_grad, text_grad)


def solution(mesh):
    in_specs = (P(AXES, None), P(AXES, None), P(), P())
    out_specs = (P(AXES, None), P(AXES, None))
    return jax.shard_map(local, mesh=mesh, in_specs=in_specs, out_specs=out_specs, check_vma=False)
```
